256 devices in a mesh: block: 16 (over x, z_hi, core), day: 16 (over y, z_lo).
Axes of the slice: x: 4, y: 4, z: 8 (z_hi: 2, z_lo: 4; z = z_hi * 4 + z_lo), core: 2. Of those that a mesh axis runs over, the one named last changes fastest.
Arguments:
- spectra: bfloat16 [16, 8, 256, 2, 4096], P('day', None, 'block'), may hold values from -6 to 6
- hour_mask: int32 [16, 8, 256], P('day', None, 'block'), may hold values 0 or 1
- pairs: int32 [16, 2], replicated, may hold values from 0 to 15, as said below
Outputs:
- correlation: float32 [16, 256, 2048], P('block', 'day')
The draws below stay inside these ranges and needn't reach their ends.
Inputs may be any that keep to these rules, and one draw needn't show every extreme that they name: `pairs`: rows k * 8 to (k + 1) * 8 - 1 form round k: every block appears in exactly one of its rows, so the two entries of a row differ.
All inputs are finite; a program needn't handle non-finite values. No bound on the sum of `hour_mask` on one device may be relied on, other than what follows from the above.
Results may differ from the reference program's by a relative error of at most 0.004.
Values may be sent and summed in bfloat16 or wider, within the bound.
No kernel may reach another device: no remote copies, remote signals or barrier semaphores. Data moves between devices by JAX's collectives and lax.ppermute only.
A program may use at most 128 MiB of HBM per device.

```python
import math
import jax
import jax.numpy as jnp
from jax import lax

F = 4096
LAGS = 2048
S_BLK = 16
HOURS = 8
ROUNDS = 2
DAYS = 16
STATIONS = 256
N_BLOCK = 16


def draw_pairs(key, part):
    rounds = []
    for index in range(ROUNDS):
        order = jax.random.permutation(jax.random.fold_in(key, 101 + index), N_BLOCK)
        rounds.append(order.astype(jnp.int32).reshape(N_BLOCK // 2, 2))
    return jnp.concatenate(rounds, axis=0)


def set_ends(entries, rng, low, largest):
    shape = entries.shape
    spot = [jax.random.randint(jax.random.fold_in(rng, axis), (), 0, shape[axis]) for axis in range(len(shape))]
    entries = entries.at[tuple(spot)].set(low)
    longest = shape.index(max(shape))
    spot[longest] = (spot[longest] + 1) % shape[longest]
    return entries.at[tuple(spot)].set(largest)


def level_of(own_key, dims, cuts, low, high):
    loudness = 1.0
    for position, blocks in cuts:
        steps = jax.random.uniform(jax.random.fold_in(jax.random.fold_in(own_key, 6), position), (blocks,), jnp.float32, low / len(cuts), high / len(cuts))
        loudness = loudness * jnp.repeat(jnp.exp(steps), dims[position] // blocks).reshape((-1,) + (1,) * (len(dims) - 1 - position))
    return loudness


def gaussian(stream_key, shape, scale, limit, pieces=(), held_as=jnp.bfloat16):
    entries = jax.random.normal(stream_key, shape, jnp.float32) * scale
    if len(pieces) > 0:
        entries = level_of(stream_key, shape, pieces, -0.22, 0.18) * entries
    return jnp.clip(entries, min=-limit, max=limit).astype(held_as)


def setup_inputs(seed: int = 0) -> dict:
    arg_keys = jax.random.split(jax.random.key(seed), 4)
    return {
        "spectra": gaussian(arg_keys[0], (DAYS, HOURS, STATIONS, 2, F), 1.0, 6.0, ((0, 16), (2, 16))),
        "hour_mask": set_ends((jax.random.randint(arg_keys[1], (DAYS, HOURS, STATIONS), 0, 4) < 3).astype(jnp.int32), jax.random.fold_in(arg_keys[1], 1), 0, 1),
        "pairs": draw_pairs(jax.random.fold_in(arg_keys[3], 71), 0),
    }


def tables(first, count, lags, width):
    bins = first + jnp.arange(count, dtype=jnp.int32)
    shifts = jnp.arange(lags, dtype=jnp.int32) - lags // 2
    turns = jnp.mod((bins + 1)[:, None] * shifts[None, :], 2 * width)
    phase = turns.astype(jnp.float32) * (math.pi / width)
    return (jnp.cos(phase), jnp.sin(phase))

def whiten_day(day_args):
    values, valid = day_args
    wide = values.astype(jnp.float32)
    power = lax.optimization_barrier(jnp.mean(wide[:, :, 0] * wide[:, :, 0] + wide[:, :, 1] * wide[:, :, 1], axis=-1))
    factor = valid.astype(jnp.float32) / jnp.sqrt(power + 1e-06)
    return (wide * factor[:, :, None, None]).astype(jnp.bfloat16)

def reference(spectra, hour_mask, pairs):
    whitened = lax.map(whiten_day, (spectra, hour_mask))
    blocks = whitened.reshape(DAYS * HOURS, N_BLOCK, S_BLK, 2, F)
    cos_table, sin_table = tables(0, F, LAGS, F)
    scale = 1.0 / math.sqrt(F * HOURS * DAYS)
    high = lax.Precision.HIGHEST

    def one_pair(pair):
        left = lax.dynamic_index_in_dim(blocks, pair[0], axis=1, keepdims=False).astype(jnp.float32)
        right = lax.dynamic_index_in_dim(blocks, pair[1], axis=1, keepdims=False).astype(jnp.float32)
        cross_re = jnp.einsum('hif,hjf->ijf', left[:, :, 0], right[:, :, 0], precision=high) + jnp.einsum('hif,hjf->ijf', left[:, :, 1], right[:, :, 1], precision=high)
        cross_im = jnp.einsum('hif,hjf->ijf', left[:, :, 1], right[:, :, 0], precision=high) - jnp.einsum('hif,hjf->ijf', left[:, :, 0], right[:, :, 1], precision=high)
        cross_re = cross_re.reshape(S_BLK * S_BLK, F)
        cross_im = cross_im.reshape(S_BLK * S_BLK, F)
        lagged = jnp.dot(cross_re, cos_table, precision=high) - jnp.dot(cross_im, sin_table, precision=high)
        return lagged * scale
    return lax.map(one_pair, pairs)
```

```python
import functools
import math

import jax
import jax.numpy as jnp
from jax import lax
from jax.experimental import pallas as pl
from jax.experimental.pallas import tpu as pltpu
from jax.sharding import PartitionSpec as P

F = 4096
LAGS = 2048
S_BLK = 16
HOURS = 8
DAYS = 16
BLOCKS = 16
PAIRS = 16
LANES = 128
TILES = F // LANES
GROUPS = 8
BINS = 16
DEVICES = 256
COARSE = 512
BOTH = ("block", "day")
VMEM = pl.BlockSpec(memory_space=pltpu.VMEM)
SMEM = pl.BlockSpec(memory_space=pltpu.SMEM)


def lane_index(shape):
    return lax.broadcasted_iota(jnp.int32, shape, len(shape) - 1)


def barrel(vectors, position):
    count = len(vectors)
    step = 1
    while step < count:
        mask = (position & step) != 0
        vectors = [jnp.where(mask, vectors[(n + step) % count], vectors[n]) for n in range(count)]
        step *= 2
    return vectors


def whiten_kernel(x_ref, mask_ref, out_ref, rows_ref, factor_ref):
    eye = lax.broadcasted_iota(jnp.int32, (S_BLK, S_BLK), 0) == lane_index((S_BLK, S_BLK))

    def hour(h, carry):
        for s in range(S_BLK):
            start = pl.multiple_of(h * (S_BLK * 64) + s * 64, 64)
            values = x_ref[pl.ds(start, 64), :].astype(jnp.float32)
            rows_ref[h, pl.ds(s, 64, stride=S_BLK), :] = values
        total = jnp.zeros((S_BLK, LANES), jnp.float32)
        for part in range(64):
            wide = rows_ref[h, part * S_BLK : (part + 1) * S_BLK, :]
            total = total + wide * wide
        power = jnp.sum(total, axis=1, keepdims=True) * (1.0 / F)
        valid = jnp.broadcast_to(mask_ref[pl.ds(h, 1), :].astype(jnp.float32), (S_BLK, S_BLK))
        valid = jnp.sum(jnp.where(eye, valid, 0.0), axis=1, keepdims=True)
        factor = valid / jnp.sqrt(power + 1e-06)
        factor_ref[h] = jnp.broadcast_to(factor, (S_BLK, LANES))
        return carry

    lax.fori_loop(0, HOURS, hour, 0)
    position = lane_index((S_BLK, LANES)) // BINS

    def part(tc, carry):
        start = pl.multiple_of(tc * S_BLK, S_BLK)
        rolled = []
        for h in range(HOURS):
            value = rows_ref[h, pl.ds(start, S_BLK), :] * factor_ref[h]
            rolled.append(pltpu.roll(value, BINS * h, 1) if h else value)
        mixed = barrel(rolled, position)
        tile = tc // 2
        side = tc % 2
        for g in range(GROUPS):
            row = pl.multiple_of((tile * GROUPS + g) * (2 * S_BLK) + side * S_BLK, S_BLK)
            out_ref[pl.ds(row, S_BLK), :] = mixed[(-g) % GROUPS].astype(jnp.bfloat16)
        return carry

    lax.fori_loop(0, 2 * TILES, part, 0)


def cross_kernel(pairs_ref, x_ref, out_ref, whole_ref, left_ref, keep_ref, flat_ref):
    position = lane_index((S_BLK, LANES)) % BINS

    def block(b, carry):
        for c in range(2):
            rolled = []
            for d in range(DAYS):
                row = pl.multiple_of((b * DAYS + d) * (2 * S_BLK) + c * S_BLK, S_BLK)
                value = x_ref[pl.ds(row, S_BLK), :].astype(jnp.float32)
                rolled.append(pltpu.roll(value, d, 1) if d else value)
            mixed = barrel(rolled, position)
            row = pl.multiple_of(b * S_BLK, S_BLK)
            for u in range(BINS):
                whole_ref[u, pl.ds(row, S_BLK), c * LANES : (c + 1) * LANES] = mixed[
                    (-u) % BINS
                ].astype(jnp.bfloat16)
        return carry

    lax.fori_loop(0, BLOCKS, block, 0)
    owner = lane_index((S_BLK, 256)) // S_BLK
    for p in range(PAIRS):
        keep_ref[p * S_BLK : (p + 1) * S_BLK, :] = (owner == pairs_ref[p, 1]).astype(jnp.float32)
    from_j = lax.broadcasted_iota(jnp.int32, (256, LANES), 0) % S_BLK
    to_lane = lane_index((256, LANES))

    def tile(t, carry):
        total = jnp.zeros((256, LANES), jnp.float32)
        for uu in range(4):
            u = t * 4 + uu
            for p in range(PAIRS):
                first = pl.multiple_of(pairs_ref[p, 0] * S_BLK, S_BLK)
                re = whole_ref[u, pl.ds(first, S_BLK), 0:LANES]
                im = whole_ref[u, pl.ds(first, S_BLK), LANES : 2 * LANES]
                here = slice(p * S_BLK, (p + 1) * S_BLK)
                there = slice(256 + p * S_BLK, 256 + (p + 1) * S_BLK)
                left_ref[here, 0:LANES] = re
                left_ref[here, LANES : 2 * LANES] = im
                left_ref[there, 0:LANES] = im
                left_ref[there, LANES : 2 * LANES] = -re
            for c in range(2):
                gram = lax.dot_general(
                    left_ref[c * 256 : (c + 1) * 256, :],
                    whole_ref[u],
                    (((1,), (1,)), ((), ())),
                    preferred_element_type=jnp.float32,
                )
                kept = (gram * keep_ref[...]).astype(jnp.bfloat16)
                place = (to_lane == from_j + (uu * 2 + c) * S_BLK).astype(jnp.bfloat16)
                total = total + jnp.dot(kept, place, preferred_element_type=jnp.float32)
        flat_ref[pl.ds(t, 256, stride=4), :] = total
        return carry

    lax.fori_loop(0, 4, tile, 0)
    out_ref[...] = flat_ref[...].astype(jnp.bfloat16)


def lag_kernel(x_ref, high_ref, low_ref, cos_ref, sin_ref, out_ref, flat_ref):
    flat_ref[...] = x_ref[...].astype(jnp.float32)
    sums = [jnp.zeros((S_BLK, COARSE), jnp.float32) for _ in range(4)]
    for t in range(4):
        part = flat_ref[pl.ds(t, 256, stride=4), :].T.astype(jnp.bfloat16)
        both = jnp.dot(part, high_ref[...], preferred_element_type=jnp.float32) + jnp.dot(
            part, low_ref[...], preferred_element_type=jnp.float32
        )
        for uu in range(4):
            re = both[uu * 32 : uu * 32 + 16]
            im = both[uu * 32 + 16 : uu * 32 + 32]
            sum_re = re[:, :COARSE] - im[:, COARSE:]
            sum_im = re[:, COARSE:] + im[:, :COARSE]
            for w in range(4):
                row = (t * 4 + uu) * 4 + w
                sums[w] = sums[w] + (
                    sum_re * cos_ref[row : row + 1, :] - sum_im * sin_ref[row : row + 1, :]
                )
    for w in range(4):
        out_ref[:, w * COARSE : (w + 1) * COARSE] = sums[w]


def coarse_tables():
    turns = jnp.arange(256, dtype=jnp.int32)[:, None] * jnp.arange(COARSE, dtype=jnp.int32)[None, :]
    phase = jnp.mod(turns, COARSE).astype(jnp.float32) * (2 * math.pi / COARSE)
    table = jnp.concatenate([jnp.cos(phase), jnp.sin(phase)], axis=1)
    high = lax.reduce_precision(table, 8, 7)
    return high.astype(jnp.bfloat16), (table - high).astype(jnp.bfloat16)


def fine_tables(scale):
    shift = (
        jnp.arange(4, dtype=jnp.int32)[:, None] * COARSE
        + jnp.arange(COARSE, dtype=jnp.int32)[None, :]
        - LAGS // 2
    )
    turns = (jnp.arange(BINS, dtype=jnp.int32) + 1)[:, None, None] * shift[None]
    phase = jnp.mod(turns, 2 * F).astype(jnp.float32) * (math.pi / F)
    phase = phase.reshape(BINS * 4, COARSE)
    return jnp.cos(phase) * scale, jnp.sin(phase) * scale


def shards(spectra, hour_mask, pairs):
    values = spectra.reshape(HOURS, S_BLK, 2, TILES, LANES).transpose(0, 1, 3, 2, 4)
    values = values.reshape(HOURS * S_BLK * TILES * 2, LANES)
    whitened = pl.pallas_call(
        whiten_kernel,
        out_shape=jax.ShapeDtypeStruct((DEVICES * 2 * S_BLK, LANES), jnp.bfloat16),
        in_specs=[VMEM, VMEM],
        out_specs=VMEM,
        scratch_shapes=[
            pltpu.VMEM((HOURS, 64 * S_BLK, LANES), jnp.float32),
            pltpu.VMEM((HOURS, S_BLK, LANES), jnp.float32),
        ],
        compiler_params=pltpu.CompilerParams(vmem_limit_bytes=40 * 1024 * 1024),
        name="whiten",
    )(values, hour_mask[0])
    spread = lax.all_to_all(
        whitened.reshape(DEVICES, 2 * S_BLK, LANES), BOTH, split_axis=0, concat_axis=0, tiled=True
    )
    cross = pl.pallas_call(
        cross_kernel,
        out_shape=jax.ShapeDtypeStruct((DEVICES * 4, LANES), jnp.bfloat16),
        in_specs=[SMEM, VMEM],
        out_specs=VMEM,
        scratch_shapes=[
            pltpu.VMEM((BINS, 256, 256), jnp.bfloat16),
            pltpu.VMEM((512, 256), jnp.bfloat16),
            pltpu.VMEM((256, 256), jnp.float32),
            pltpu.VMEM((DEVICES * 4, LANES), jnp.float32),
        ],
        compiler_params=pltpu.CompilerParams(vmem_limit_bytes=40 * 1024 * 1024),
        name="cross",
    )(pairs, spread.reshape(DEVICES * 2 * S_BLK, LANES))
    owned = lax.all_to_all(
        cross.reshape(DEVICES, 4, LANES), BOTH, split_axis=0, concat_axis=0, tiled=True
    )
    high, low = coarse_tables()
    cos_fine, sin_fine = fine_tables(1.0 / math.sqrt(F * HOURS * DAYS))
    result = pl.pallas_call(
        lag_kernel,
        out_shape=jax.ShapeDtypeStruct((S_BLK, LAGS), jnp.float32),
        in_specs=[VMEM] * 5,
        out_specs=VMEM,
        scratch_shapes=[pltpu.VMEM((DEVICES * 4, LANES), jnp.float32)],
        compiler_params=pltpu.CompilerParams(vmem_limit_bytes=40 * 1024 * 1024),
        name="lag",
    )(owned.reshape(DEVICES * 4, LANES), high, low, cos_fine, sin_fine)
    return result.reshape(1, S_BLK, LAGS)


def solution(mesh):
    in_specs = (P("day", None, "block", None, None), P("day", None, "block"), P())
    out_specs = P("block", "day", None)
    return jax.shard_map(shards, mesh=mesh, in_specs=in_specs, out_specs=out_specs, check_vma=False)
```

```python
import math

import jax
import jax.numpy as jnp
from jax import lax
from jax.experimental import pallas as pl
from jax.experimental.pallas import tpu as pltpu
from jax.sharding import PartitionSpec as P

F = 4096
LAGS = 2048
S_BLK = 16
HOURS = 8
DAYS = 16
BLOCKS = 16
PAIRS = 16
LANES = 128
TILES = F // LANES
GROUPS = 8
BINS = 16
DEVICES = 256
COARSE = 512
BOTH = ("block", "day")
VMEM = pl.BlockSpec(memory_space=pltpu.VMEM)
SMEM = pl.BlockSpec(memory_space=pltpu.SMEM)


def lane_index(shape):
    return lax.broadcasted_iota(jnp.int32, shape, len(shape) - 1)


def barrel(vectors, position):
    count = len(vectors)
    step = 1
    while step < count:
        mask = (position & step) != 0
        vectors = [jnp.where(mask, vectors[(n + step) % count], vectors[n]) for n in range(count)]
        step *= 2
    return vectors


def whiten_kernel(x_ref, mask_ref, out_ref, rows_ref, factor_ref):
    step = pl.program_id(0)

    @pl.when(step < HOURS)
    def _():
        for s in range(S_BLK):
            values = x_ref[s * 64 : (s + 1) * 64, :].astype(jnp.float32)
            rows_ref[step, pl.ds(s, 64, stride=S_BLK), :] = values
        totals = [jnp.zeros((S_BLK, LANES), jnp.float32) for _ in range(4)]
        for part in range(64):
            wide = rows_ref[step, part * S_BLK : (part + 1) * S_BLK, :]
            totals[part % 4] = totals[part % 4] + wide * wide
        total = (totals[0] + totals[1]) + (totals[2] + totals[3])
        power = jnp.sum(total, axis=1, keepdims=True) * (1.0 / F)
        eye = lax.broadcasted_iota(jnp.int32, (S_BLK, S_BLK), 0) == lane_index((S_BLK, S_BLK))
        valid = jnp.broadcast_to(mask_ref[pl.ds(step, 1), :].astype(jnp.float32), (S_BLK, S_BLK))
        valid = jnp.sum(jnp.where(eye, valid, 0.0), axis=1, keepdims=True)
        factor = valid / jnp.sqrt(power + 1e-06)
        factor_ref[step] = jnp.broadcast_to(factor, (S_BLK, LANES))

    @pl.when(step >= HOURS)
    def _():
        position = lane_index((S_BLK, LANES)) // BINS
        first = (step - HOURS) * 16
        for part in range(16):
            start = pl.multiple_of((first + part) * S_BLK, S_BLK)
            rolled = []
            for h in range(HOURS):
                value = (rows_ref[h, pl.ds(start, S_BLK), :] * factor_ref[h]).astype(jnp.bfloat16)
                rolled.append(pltpu.roll(value, BINS * h, 1) if h else value)
            mixed = barrel(rolled, position)
            for g in range(GROUPS):
                row = (part // 2 * GROUPS + g) * (2 * S_BLK) + part % 2 * S_BLK
                out_ref[row : row + S_BLK, :] = mixed[(-g) % GROUPS]


def cross_kernel(pairs_ref, x_ref, out_ref, whole_ref, keep_ref, flat_ref):
    position = lane_index((S_BLK, LANES)) % BINS

    def block(step, carry):
        for k in range(2):
            b = step * 2 + k
            for c in range(2):
                rolled = []
                for d in range(DAYS):
                    row = pl.multiple_of((b * DAYS + d) * (2 * S_BLK) + c * S_BLK, S_BLK)
                    value = x_ref[pl.ds(row, S_BLK), :]
                    rolled.append(pltpu.roll(value, d, 1) if d else value)
                mixed = barrel(rolled, position)
                row = pl.multiple_of(b * S_BLK, S_BLK)
                for u in range(BINS):
                    whole_ref[u, pl.ds(row, S_BLK), c * LANES : (c + 1) * LANES] = mixed[(-u) % BINS]
        return carry

    lax.fori_loop(0, BLOCKS // 2, block, 0)
    owner = lane_index((S_BLK, 256)) // S_BLK
    for p in range(PAIRS):
        keep_ref[p * S_BLK : (p + 1) * S_BLK, :] = (owner == pairs_ref[p, 1]).astype(jnp.float32)
    from_j = lax.broadcasted_iota(jnp.int32, (256, LANES), 0) % S_BLK
    to_lane = lane_index((256, LANES))
    firsts = [pl.multiple_of(pairs_ref[p, 0] * S_BLK, S_BLK) for p in range(PAIRS)]
    for t in range(4):
        total = jnp.zeros((256, LANES), jnp.float32)
        for uu in range(4):
            u = t * 4 + uu
            re, im = (
                jnp.concatenate(
                    [whole_ref[u, pl.ds(first, S_BLK), c * LANES : (c + 1) * LANES] for first in firsts],
                    axis=0,
                )
                for c in range(2)
            )
            right = whole_ref[u]
            for c in range(2):
                left = jnp.concatenate([im, -re] if c else [re, im], axis=1)
                gram = lax.dot_general(
                    left, right, (((1,), (1,)), ((), ())), preferred_element_type=jnp.float32
                )
                kept = (gram * keep_ref[...]).astype(jnp.bfloat16)
                place = (to_lane == from_j + (uu * 2 + c) * S_BLK).astype(jnp.bfloat16)
                total = total + jnp.dot(kept, place, preferred_element_type=jnp.float32)
        flat_ref[pl.ds(t, 256, stride=4), :] = total
    out_ref[...] = flat_ref[...].astype(jnp.bfloat16)


def lag_kernel(x_ref, high_ref, low_ref, cos_ref, sin_ref, out_ref, flat_ref):
    flat_ref[...] = x_ref[...].astype(jnp.float32)
    sums = [jnp.zeros((S_BLK, COARSE), jnp.float32) for _ in range(4)]
    for t in range(4):
        part = flat_ref[pl.ds(t, 256, stride=4), :].T.astype(jnp.bfloat16)
        both = jnp.dot(part, high_ref[...], preferred_element_type=jnp.float32) + jnp.dot(
            part, low_ref[...], preferred_element_type=jnp.float32
        )
        for uu in range(4):
            re = both[uu * 32 : uu * 32 + 16]
            im = both[uu * 32 + 16 : uu * 32 + 32]
            sum_re = re[:, :COARSE] - im[:, COARSE:]
            sum_im = re[:, COARSE:] + im[:, :COARSE]
            for w in range(4):
                row = (t * 4 + uu) * 4 + w
                sums[w] = sums[w] + (
                    sum_re * cos_ref[row : row + 1, :] - sum_im * sin_ref[row : row + 1, :]
                )
    for w in range(4):
        out_ref[:, w * COARSE : (w + 1) * COARSE] = sums[w]


def coarse_tables():
    turns = jnp.arange(256, dtype=jnp.int32)[:, None] * jnp.arange(COARSE, dtype=jnp.int32)[None, :]
    phase = jnp.mod(turns, COARSE).astype(jnp.float32) * (2 * math.pi / COARSE)
    table = jnp.concatenate([jnp.cos(phase), jnp.sin(phase)], axis=1)
    high = lax.reduce_precision(table, 8, 7)
    return high.astype(jnp.bfloat16), (table - high).astype(jnp.bfloat16)


def fine_tables(scale):
    shift = (
        jnp.arange(4, dtype=jnp.int32)[:, None] * COARSE
        + jnp.arange(COARSE, dtype=jnp.int32)[None, :]
        - LAGS // 2
    )
    turns = (jnp.arange(BINS, dtype=jnp.int32) + 1)[:, None, None] * shift[None]
    phase = jnp.mod(turns, 2 * F).astype(jnp.float32) * (math.pi / F)
    phase = phase.reshape(BINS * 4, COARSE)
    return jnp.cos(phase) * scale, jnp.sin(phase) * scale


def shards(spectra, hour_mask, pairs):
    values = spectra.reshape(HOURS, S_BLK, 2, TILES, LANES).transpose(0, 1, 3, 2, 4)
    values = values.reshape(HOURS * S_BLK * TILES * 2, LANES)
    whitened = pl.pallas_call(
        whiten_kernel,
        out_shape=jax.ShapeDtypeStruct((DEVICES * 2 * S_BLK, LANES), jnp.bfloat16),
        grid=(HOURS + 4,),
        in_specs=[
            pl.BlockSpec((S_BLK * 64, LANES), lambda i: (jnp.minimum(i, HOURS - 1), 0)),
            pl.BlockSpec((HOURS, S_BLK), lambda i: (0, 0)),
        ],
        out_specs=pl.BlockSpec((DEVICES * S_BLK // 2, LANES), lambda i: (jnp.maximum(i - HOURS, 0), 0)),
        scratch_shapes=[
            pltpu.VMEM((HOURS, 64 * S_BLK, LANES), jnp.float32),
            pltpu.VMEM((HOURS, S_BLK, LANES), jnp.float32),
        ],
        compiler_params=pltpu.CompilerParams(vmem_limit_bytes=40 * 1024 * 1024),
        name="whiten",
    )(values, hour_mask[0])
    spread = lax.all_to_all(
        whitened.reshape(DEVICES, 2 * S_BLK, LANES), BOTH, split_axis=0, concat_axis=0, tiled=True
    )
    cross = pl.pallas_call(
        cross_kernel,
        out_shape=jax.ShapeDtypeStruct((DEVICES * 4, LANES), jnp.bfloat16),
        in_specs=[SMEM, VMEM],
        out_specs=VMEM,
        scratch_shapes=[
            pltpu.VMEM((BINS, 256, 256), jnp.bfloat16),
            pltpu.VMEM((256, 256), jnp.float32),
            pltpu.VMEM((DEVICES * 4, LANES), jnp.float32),
        ],
        compiler_params=pltpu.CompilerParams(vmem_limit_bytes=40 * 1024 * 1024),
        name="cross",
    )(pairs, spread.reshape(DEVICES * 2 * S_BLK, LANES))
    owned = lax.all_to_all(
        cross.reshape(DEVICES, 4, LANES), BOTH, split_axis=0, concat_axis=0, tiled=True
    )
    high, low = coarse_tables()
    cos_fine, sin_fine = fine_tables(1.0 / math.sqrt(F * HOURS * DAYS))
    result = pl.pallas_call(
        lag_kernel,
        out_shape=jax.ShapeDtypeStruct((S_BLK, LAGS), jnp.float32),
        in_specs=[VMEM] * 5,
        out_specs=VMEM,
        scratch_shapes=[pltpu.VMEM((DEVICES * 4, LANES), jnp.float32)],
        compiler_params=pltpu.CompilerParams(vmem_limit_bytes=40 * 1024 * 1024),
        name="lag",
    )(owned.reshape(DEVICES * 4, LANES), high, low, cos_fine, sin_fine)
    return result.reshape(1, S_BLK, LAGS)


def solution(mesh):
    in_specs = (P("day", None, "block", None, None), P("day", None, "block"), P())
    out_specs = P("block", "day", None)
    return jax.shard_map(shards, mesh=mesh, in_specs=in_specs, out_specs=out_specs, check_vma=False)
```

```python
import math

import jax
import jax.numpy as jnp
from jax import lax
from jax.experimental import pallas as pl
from jax.experimental.pallas import tpu as pltpu
from jax.sharding import PartitionSpec as P

F = 4096
LAGS = 2048
S_BLK = 16
HOURS = 8
DAYS = 16
BLOCKS = 16
PAIRS = 16
LANES = 128
TILES = F // LANES
GROUPS = 8
BINS = 16
DEVICES = 256
COARSE = 512
ROWS = 24
QUARTER = DEVICES * 2 * S_BLK // 4
BOTH = ("block", "day")
VMEM = pl.BlockSpec(memory_space=pltpu.VMEM)
ANY = pl.BlockSpec(memory_space=pl.ANY)
SMEM = pl.BlockSpec(memory_space=pltpu.SMEM)


def lane_index(shape):
    return lax.broadcasted_iota(jnp.int32, shape, len(shape) - 1)


def barrel(vectors, position):
    count = len(vectors)
    step = 1
    while step < count:
        mask = (position & step) != 0
        vectors = [jnp.where(mask, vectors[(n + step) % count], vectors[n]) for n in range(count)]
        step *= 2
    return vectors


def whiten_kernel(
    x_hbm, mask_hbm, out_hbm, x_ref, mask_ref, rows_ref, factor_ref, out_ref, in_sem, mask_sem, out_sem
):
    def read(h):
        here = x_hbm.at[pl.ds(h * S_BLK * 64, S_BLK * 64)]
        return pltpu.make_async_copy(here, x_ref.at[h], in_sem.at[h])

    def write(q):
        here = pl.ds(q * QUARTER, QUARTER)
        return pltpu.make_async_copy(out_ref.at[here], out_hbm.at[here], out_sem.at[q])

    for h in range(HOURS):
        read(h).start()
    mask_copy = pltpu.make_async_copy(mask_hbm, mask_ref, mask_sem)
    mask_copy.start()
    mask_copy.wait()
    eye = lax.broadcasted_iota(jnp.int32, (S_BLK, S_BLK), 0) == lane_index((S_BLK, S_BLK))
    for h in range(HOURS):
        read(h).wait()
        for s in range(S_BLK):
            values = x_ref[h, s * 64 : (s + 1) * 64, :]
            if h:
                values = pltpu.roll(values, BINS * h, 1)
            rows_ref[h, pl.ds(s, 64, stride=ROWS), :] = values.astype(jnp.float32)
        totals = [jnp.zeros((S_BLK, LANES), jnp.float32) for _ in range(4)]
        for part in range(64):
            wide = rows_ref[h, part * ROWS : part * ROWS + S_BLK, :]
            totals[part % 4] = totals[part % 4] + wide * wide
        total = (totals[0] + totals[1]) + (totals[2] + totals[3])
        power = jnp.sum(total, axis=1, keepdims=True) * (1.0 / F)
        valid = jnp.broadcast_to(mask_ref[h : h + 1, :].astype(jnp.float32), (S_BLK, S_BLK))
        valid = jnp.sum(jnp.where(eye, valid, 0.0), axis=1, keepdims=True)
        factor_ref[h] = jnp.broadcast_to(valid / jnp.sqrt(power + 1e-06), (S_BLK, LANES))
    position = lane_index((S_BLK, LANES)) // BINS

    def quarter(q, carry):
        for part in range(16):
            start = pl.multiple_of((q * 16 + part) * ROWS, 8)
            rolled = [
                (rows_ref[h, pl.ds(start, S_BLK), :] * factor_ref[h]).astype(jnp.bfloat16)
                for h in range(HOURS)
            ]
            mixed = barrel(rolled, position)
            for g in range(GROUPS):
                row = (part // 2 * GROUPS + g) * (2 * S_BLK) + part % 2 * S_BLK
                row = pl.multiple_of(q * QUARTER + row, S_BLK)
                out_ref[pl.ds(row, S_BLK), :] = mixed[(-g) % GROUPS]
        write(q).start()
        return carry

    lax.fori_loop(0, 4, quarter, 0)
    for q in range(4):
        write(q).wait()


def cross_kernel(pairs_ref, x_ref, out_ref, whole_ref, keep_ref, place_ref, flat_ref):
    position = lane_index((S_BLK, LANES)) % BINS
    for b in range(BLOCKS):
        for c in range(2):
            rolled = []
            for d in range(DAYS):
                row = (b * DAYS + d) * (2 * S_BLK) + c * S_BLK
                value = x_ref[row : row + S_BLK, :]
                rolled.append(pltpu.roll(value, d, 1) if d else value)
            mixed = barrel(rolled, position)
            for u in range(BINS):
                whole_ref[u, b * S_BLK : (b + 1) * S_BLK, c * LANES : (c + 1) * LANES] = mixed[
                    (-u) % BINS
                ]
    owner = lane_index((S_BLK, 256)) // S_BLK
    for p in range(PAIRS):
        kept = (owner == pairs_ref[p, 1]).astype(jnp.float32)
        keep_ref[p * S_BLK : (p + 1) * S_BLK, :] = kept.astype(jnp.bfloat16)
    from_j = lax.broadcasted_iota(jnp.int32, (LANES, LANES), 0) % S_BLK
    to_lane = lane_index((LANES, LANES))
    for n in range(8):
        placed = (to_lane == from_j + n * S_BLK).astype(jnp.float32)
        place_ref[n * LANES : (n + 1) * LANES, :] = placed.astype(jnp.bfloat16)
    firsts = [pl.multiple_of(pairs_ref[p, 0] * S_BLK, S_BLK) for p in range(PAIRS)]
    for t in range(4):
        folded = []
        for uu in range(4):
            u = t * 4 + uu
            re, im = (
                jnp.concatenate(
                    [whole_ref[u, pl.ds(first, S_BLK), c * LANES : (c + 1) * LANES] for first in firsts],
                    axis=0,
                )
                for c in range(2)
            )
            right = whole_ref[u]
            for c in range(2):
                left = jnp.concatenate([im, -re] if c else [re, im], axis=1)
                gram = lax.dot_general(
                    left, right, (((1,), (1,)), ((), ())), preferred_element_type=jnp.float32
                )
                kept = gram.astype(jnp.bfloat16) * keep_ref[...]
                folded.append(kept[:, :LANES] + kept[:, LANES:])
        flat_ref[pl.ds(t, 256, stride=4), :] = jnp.dot(
            jnp.concatenate(folded, axis=1), place_ref[...], preferred_element_type=jnp.float32
        )
    out_ref[...] = flat_ref[...].astype(jnp.bfloat16)


def lag_kernel(x_ref, high_ref, low_ref, cos_ref, sin_ref, out_ref, flat_ref):
    flat_ref[...] = x_ref[...].astype(jnp.float32)
    sums = [jnp.zeros((S_BLK, COARSE), jnp.float32) for _ in range(4)]
    for t in range(4):
        part = flat_ref[pl.ds(t, 256, stride=4), :].T.astype(jnp.bfloat16)
        both = jnp.dot(part, high_ref[...], preferred_element_type=jnp.float32) + jnp.dot(
            part, low_ref[...], preferred_element_type=jnp.float32
        )
        for uu in range(4):
            re = both[uu * 32 : uu * 32 + 16]
            im = both[uu * 32 + 16 : uu * 32 + 32]
            sum_re = re[:, :COARSE] - im[:, COARSE:]
            sum_im = re[:, COARSE:] + im[:, :COARSE]
            for w in range(4):
                row = (t * 4 + uu) * 4 + w
                sums[w] = sums[w] + (
                    sum_re * cos_ref[row : row + 1, :] - sum_im * sin_ref[row : row + 1, :]
                )
    for w in range(4):
        out_ref[:, w * COARSE : (w + 1) * COARSE] = sums[w]


def coarse_tables():
    turns = jnp.arange(256, dtype=jnp.int32)[:, None] * jnp.arange(COARSE, dtype=jnp.int32)[None, :]
    phase = jnp.mod(turns, COARSE).astype(jnp.float32) * (2 * math.pi / COARSE)
    table = jnp.concatenate([jnp.cos(phase), jnp.sin(phase)], axis=1)
    high = lax.reduce_precision(table, 8, 7)
    return high.astype(jnp.bfloat16), (table - high).astype(jnp.bfloat16)


def fine_tables(scale):
    shift = (
        jnp.arange(4, dtype=jnp.int32)[:, None] * COARSE
        + jnp.arange(COARSE, dtype=jnp.int32)[None, :]
        - LAGS // 2
    )
    turns = (jnp.arange(BINS, dtype=jnp.int32) + 1)[:, None, None] * shift[None]
    phase = jnp.mod(turns, 2 * F).astype(jnp.float32) * (math.pi / F)
    phase = phase.reshape(BINS * 4, COARSE)
    return jnp.cos(phase) * scale, jnp.sin(phase) * scale


def shards(spectra, hour_mask, pairs):
    values = spectra.reshape(HOURS, S_BLK, 2, TILES, LANES).transpose(0, 1, 3, 2, 4)
    values = values.reshape(HOURS * S_BLK * TILES * 2, LANES)
    whitened = pl.pallas_call(
        whiten_kernel,
        out_shape=jax.ShapeDtypeStruct((DEVICES * 2 * S_BLK, LANES), jnp.bfloat16),
        in_specs=[ANY, ANY],
        out_specs=ANY,
        scratch_shapes=[
            pltpu.VMEM((HOURS, S_BLK * 64, LANES), jnp.bfloat16),
            pltpu.VMEM((HOURS, S_BLK), jnp.int32),
            pltpu.VMEM((HOURS, 64 * ROWS, LANES), jnp.float32),
            pltpu.VMEM((HOURS, S_BLK, LANES), jnp.float32),
            pltpu.VMEM((DEVICES * 2 * S_BLK, LANES), jnp.bfloat16),
            pltpu.SemaphoreType.DMA((HOURS,)),
            pltpu.SemaphoreType.DMA,
            pltpu.SemaphoreType.DMA((4,)),
        ],
        compiler_params=pltpu.CompilerParams(vmem_limit_bytes=60 * 1024 * 1024),
        name="whiten",
    )(values, hour_mask[0])
    spread = lax.all_to_all(
        whitened.reshape(DEVICES, 2 * S_BLK, LANES), BOTH, split_axis=0, concat_axis=0, tiled=True
    )
    cross = pl.pallas_call(
        cross_kernel,
        out_shape=jax.ShapeDtypeStruct((DEVICES * 4, LANES), jnp.bfloat16),
        in_specs=[SMEM, VMEM],
        out_specs=VMEM,
        scratch_shapes=[
            pltpu.VMEM((BINS, 256, 256), jnp.bfloat16),
            pltpu.VMEM((256, 256), jnp.bfloat16),
            pltpu.VMEM((8 * LANES, LANES), jnp.bfloat16),
            pltpu.VMEM((DEVICES * 4, LANES), jnp.float32),
        ],
        compiler_params=pltpu.CompilerParams(vmem_limit_bytes=40 * 1024 * 1024),
        name="cross",
    )(pairs, spread.reshape(DEVICES * 2 * S_BLK, LANES))
    owned = lax.all_to_all(
        cross.reshape(DEVICES, 4, LANES), BOTH, split_axis=0, concat_axis=0, tiled=True
    )
    high, low = coarse_tables()
    cos_fine, sin_fine = fine_tables(1.0 / math.sqrt(F * HOURS * DAYS))
    result = pl.pallas_call(
        lag_kernel,
        out_shape=jax.ShapeDtypeStruct((S_BLK, LAGS), jnp.float32),
        in_specs=[VMEM] * 5,
        out_specs=VMEM,
        scratch_shapes=[pltpu.VMEM((DEVICES * 4, LANES), jnp.float32)],
        compiler_params=pltpu.CompilerParams(vmem_limit_bytes=40 * 1024 * 1024),
        name="lag",
    )(owned.reshape(DEVICES * 4, LANES), high, low, cos_fine, sin_fine)
    return result.reshape(1, S_BLK, LAGS)


def solution(mesh):
    in_specs = (P("day", None, "block", None, None), P("day", None, "block"), P())
    out_specs = P("block", "day", None)
    return jax.shard_map(shards, mesh=mesh, in_specs=in_specs, out_specs=out_specs, check_vma=False)
```

```python
import math

import jax
import jax.numpy as jnp
from jax import lax
from jax.experimental import pallas as pl
from jax.experimental.pallas import tpu as pltpu
from jax.sharding import PartitionSpec as P

F = 4096
LAGS = 2048
S_BLK = 16
HOURS = 8
DAYS = 16
BLOCKS = 16
PAIRS = 16
LANES = 128
TILES = F // LANES
GROUPS = 8
BINS = 16
DEVICES = 256
COARSE = 512
ROWS = 24
QUARTER = DEVICES * 2 * S_BLK // 4
BOTH = ("block", "day")
VMEM = pl.BlockSpec(memory_space=pltpu.VMEM)
ANY = pl.BlockSpec(memory_space=pl.ANY)
SMEM = pl.BlockSpec(memory_space=pltpu.SMEM)


def lane_index(shape):
    return lax.broadcasted_iota(jnp.int32, shape, len(shape) - 1)


def barrel(vectors, position):
    count = len(vectors)
    step = 1
    while step < count:
        mask = (position & step) != 0
        vectors = [jnp.where(mask, vectors[(n + step) % count], vectors[n]) for n in range(count)]
        step *= 2
    return vectors


def whiten_kernel(
    x_hbm,
    mask_hbm,
    out_hbm,
    x_ref,
    mask_ref,
    rows_ref,
    factor_ref,
    valid_ref,
    out_ref,
    in_sem,
    mask_sem,
    out_sem,
):
    def read(h):
        here = x_hbm.at[pl.ds(h * S_BLK * 64, S_BLK * 64)]
        return pltpu.make_async_copy(here, x_ref.at[h], in_sem.at[h])

    def write(q):
        here = pl.ds(q * QUARTER, QUARTER)
        return pltpu.make_async_copy(out_ref.at[here], out_hbm.at[here], out_sem.at[q])

    mask_copy = pltpu.make_async_copy(mask_hbm, mask_ref, mask_sem)
    mask_copy.start()
    for h in range(HOURS):
        read(h).start()
    mask_copy.wait()
    eye = lax.broadcasted_iota(jnp.int32, (S_BLK, S_BLK), 0) == lane_index((S_BLK, S_BLK))
    for h in range(HOURS):
        valid = jnp.broadcast_to(mask_ref[h : h + 1, :].astype(jnp.float32), (S_BLK, S_BLK))
        valid = jnp.sum(jnp.where(eye, valid, 0.0), axis=1, keepdims=True)
        valid_ref[h * S_BLK : (h + 1) * S_BLK, :] = jnp.broadcast_to(valid, (S_BLK, LANES))
    for h in range(HOURS):
        read(h).wait()
        totals = []
        for s in range(S_BLK):
            values = x_ref[h, s * 64 : (s + 1) * 64, :]
            if h:
                values = pltpu.roll(values, BINS * h, 1)
            wide = values.astype(jnp.float32)
            rows_ref[h, pl.ds(s, 64, stride=ROWS), :] = wide
            squares = wide * wide
            total = squares[0:8]
            for r in range(1, 8):
                total = total + squares[r * 8 : (r + 1) * 8]
            totals.append(jnp.sum(total, axis=0, keepdims=True))
        factor_ref[h * S_BLK : (h + 1) * S_BLK, :] = jnp.concatenate(totals, axis=0)
    power = jnp.sum(factor_ref[...], axis=1, keepdims=True) * (1.0 / F)
    power = jnp.broadcast_to(power, (HOURS * S_BLK, LANES))
    factor_ref[...] = valid_ref[...] / jnp.sqrt(power + 1e-06)
    position = lane_index((S_BLK, LANES)) // BINS

    def quarter(q, carry):
        for part in range(16):
            start = pl.multiple_of((q * 16 + part) * ROWS, 8)
            rolled = [
                (rows_ref[h, pl.ds(start, S_BLK), :] * factor_ref[h * S_BLK : (h + 1) * S_BLK, :]).astype(
                    jnp.bfloat16
                )
                for h in range(HOURS)
            ]
            mixed = barrel(rolled, position)
            for g in range(GROUPS):
                row = (part // 2 * GROUPS + g) * (2 * S_BLK) + part % 2 * S_BLK
                row = pl.multiple_of(q * QUARTER + row, S_BLK)
                out_ref[pl.ds(row, S_BLK), :] = mixed[(-g) % GROUPS]
        write(q).start()
        return carry

    lax.fori_loop(0, 4, quarter, 0)
    for q in range(4):
        write(q).wait()


def cross_kernel(pairs_ref, x_ref, out_ref, whole_ref, keep_ref, place_ref, flat_ref):
    position = lane_index((S_BLK, LANES)) % BINS
    for b in range(BLOCKS):
        for c in range(2):
            rolled = []
            for d in range(DAYS):
                row = (b * DAYS + d) * (2 * S_BLK) + c * S_BLK
                value = x_ref[row : row + S_BLK, :]
                rolled.append(pltpu.roll(value, d, 1) if d else value)
            mixed = barrel(rolled, position)
            for u in range(BINS):
                whole_ref[u, b * S_BLK : (b + 1) * S_BLK, c * LANES : (c + 1) * LANES] = mixed[
                    (-u) % BINS
                ]
    owner = lane_index((S_BLK, 256)) // S_BLK
    for p in range(PAIRS):
        kept = (owner == pairs_ref[p, 1]).astype(jnp.float32)
        keep_ref[p * S_BLK : (p + 1) * S_BLK, :] = kept.astype(jnp.bfloat16)
    from_j = lax.broadcasted_iota(jnp.int32, (LANES, LANES), 0) % S_BLK
    to_lane = lane_index((LANES, LANES))
    for n in range(8):
        placed = (to_lane == from_j + n * S_BLK).astype(jnp.float32)
        place_ref[n * LANES : (n + 1) * LANES, :] = placed.astype(jnp.bfloat16)
    firsts = [pl.multiple_of(pairs_ref[p, 0] * S_BLK, S_BLK) for p in range(PAIRS)]
    for t in range(4):
        folded = []
        for uu in range(4):
            u = t * 4 + uu
            re, im = (
                jnp.concatenate(
                    [whole_ref[u, pl.ds(first, S_BLK), c * LANES : (c + 1) * LANES] for first in firsts],
                    axis=0,
                )
                for c in range(2)
            )
            right = whole_ref[u]
            for c in range(2):
                left = jnp.concatenate([im, -re] if c else [re, im], axis=1)
                gram = lax.dot_general(
                    left, right, (((1,), (1,)), ((), ())), preferred_element_type=jnp.float32
                )
                kept = gram.astype(jnp.bfloat16) * keep_ref[...]
                folded.append(kept[:, :LANES] + kept[:, LANES:])
        flat_ref[pl.ds(t, 256, stride=4), :] = jnp.dot(
            jnp.concatenate(folded, axis=1), place_ref[...], preferred_element_type=jnp.float32
        )
    out_ref[...] = flat_ref[...].astype(jnp.bfloat16)


def lag_kernel(x_ref, high_ref, low_ref, cos_ref, sin_ref, out_ref, flat_ref):
    flat_ref[...] = x_ref[...].astype(jnp.float32)
    sums = [jnp.zeros((S_BLK, COARSE), jnp.float32) for _ in range(4)]
    for t in range(4):
        part = flat_ref[pl.ds(t, 256, stride=4), :].T.astype(jnp.bfloat16)
        both = jnp.dot(part, high_ref[...], preferred_element_type=jnp.float32) + jnp.dot(
            part, low_ref[...], preferred_element_type=jnp.float32
        )
        for uu in range(4):
            re = both[uu * 32 : uu * 32 + 16]
            im = both[uu * 32 + 16 : uu * 32 + 32]
            sum_re = re[:, :COARSE] - im[:, COARSE:]
            sum_im = re[:, COARSE:] + im[:, :COARSE]
            for w in range(4):
                row = (t * 4 + uu) * 4 + w
                sums[w] = sums[w] + (
                    sum_re * cos_ref[row : row + 1, :] - sum_im * sin_ref[row : row + 1, :]
                )
    for w in range(4):
        out_ref[:, w * COARSE : (w + 1) * COARSE] = sums[w]


def coarse_tables():
    turns = jnp.arange(256, dtype=jnp.int32)[:, None] * jnp.arange(COARSE, dtype=jnp.int32)[None, :]
    phase = jnp.mod(turns, COARSE).astype(jnp.float32) * (2 * math.pi / COARSE)
    table = jnp.concatenate([jnp.cos(phase), jnp.sin(phase)], axis=1)
    high = lax.reduce_precision(table, 8, 7)
    return high.astype(jnp.bfloat16), (table - high).astype(jnp.bfloat16)


def fine_tables(scale):
    shift = (
        jnp.arange(4, dtype=jnp.int32)[:, None] * COARSE
        + jnp.arange(COARSE, dtype=jnp.int32)[None, :]
        - LAGS // 2
    )
    turns = (jnp.arange(BINS, dtype=jnp.int32) + 1)[:, None, None] * shift[None]
    phase = jnp.mod(turns, 2 * F).astype(jnp.float32) * (math.pi / F)
    phase = phase.reshape(BINS * 4, COARSE)
    return jnp.cos(phase) * scale, jnp.sin(phase) * scale


def shards(spectra, hour_mask, pairs):
    values = spectra.reshape(HOURS, S_BLK, 2, TILES, LANES).transpose(0, 1, 3, 2, 4)
    values = values.reshape(HOURS * S_BLK * TILES * 2, LANES)
    whitened = pl.pallas_call(
        whiten_kernel,
        out_shape=jax.ShapeDtypeStruct((DEVICES * 2 * S_BLK, LANES), jnp.bfloat16),
        in_specs=[ANY, ANY],
        out_specs=ANY,
        scratch_shapes=[
            pltpu.VMEM((HOURS, S_BLK * 64, LANES), jnp.bfloat16),
            pltpu.VMEM((HOURS, S_BLK), jnp.int32),
            pltpu.VMEM((HOURS, 64 * ROWS, LANES), jnp.float32),
            pltpu.VMEM((HOURS * S_BLK, LANES), jnp.float32),
            pltpu.VMEM((HOURS * S_BLK, LANES), jnp.float32),
            pltpu.VMEM((DEVICES * 2 * S_BLK, LANES), jnp.bfloat16),
            pltpu.SemaphoreType.DMA((HOURS,)),
            pltpu.SemaphoreType.DMA,
            pltpu.SemaphoreType.DMA((4,)),
        ],
        compiler_params=pltpu.CompilerParams(vmem_limit_bytes=60 * 1024 * 1024),
        name="whiten",
    )(values, hour_mask[0])
    spread = lax.all_to_all(
        whitened.reshape(DEVICES, 2 * S_BLK, LANES), BOTH, split_axis=0, concat_axis=0, tiled=True
    )
    cross = pl.pallas_call(
        cross_kernel,
        out_shape=jax.ShapeDtypeStruct((DEVICES * 4, LANES), jnp.bfloat16),
        in_specs=[SMEM, VMEM],
        out_specs=VMEM,
        scratch_shapes=[
            pltpu.VMEM((BINS, 256, 256), jnp.bfloat16),
            pltpu.VMEM((256, 256), jnp.bfloat16),
            pltpu.VMEM((8 * LANES, LANES), jnp.bfloat16),
            pltpu.VMEM((DEVICES * 4, LANES), jnp.float32),
        ],
        compiler_params=pltpu.CompilerParams(vmem_limit_bytes=40 * 1024 * 1024),
        name="cross",
    )(pairs, spread.reshape(DEVICES * 2 * S_BLK, LANES))
    owned = lax.all_to_all(
        cross.reshape(DEVICES, 4, LANES), BOTH, split_axis=0, concat_axis=0, tiled=True
    )
    high, low = coarse_tables()
    cos_fine, sin_fine = fine_tables(1.0 / math.sqrt(F * HOURS * DAYS))
    result = pl.pallas_call(
        lag_kernel,
        out_shape=jax.ShapeDtypeStruct((S_BLK, LAGS), jnp.float32),
        in_specs=[VMEM] * 5,
        out_specs=VMEM,
        scratch_shapes=[pltpu.VMEM((DEVICES * 4, LANES), jnp.float32)],
        compiler_params=pltpu.CompilerParams(vmem_limit_bytes=40 * 1024 * 1024),
        name="lag",
    )(owned.reshape(DEVICES * 4, LANES), high, low, cos_fine, sin_fine)
    return result.reshape(1, S_BLK, LAGS)


def solution(mesh):
    in_specs = (P("day", None, "block", None, None), P("day", None, "block"), P())
    out_specs = P("block", "day", None)
    return jax.shard_map(shards, mesh=mesh, in_specs=in_specs, out_specs=out_specs, check_vma=False)
```

```python
import math

import jax
import jax.numpy as jnp
from jax import lax
from jax.experimental import pallas as pl
from jax.experimental.pallas import tpu as pltpu
from jax.sharding import PartitionSpec as P

F = 4096
LAGS = 2048
S_BLK = 16
HOURS = 8
DAYS = 16
BLOCKS = 16
PAIRS = 16
LANES = 128
TILES = F // LANES
GROUPS = 8
BINS = 16
DEVICES = 256
COARSE = 512
PITCH = 72
QUARTER = DEVICES * 2 * S_BLK // 4
BOTH = ("block", "day")
VMEM = pl.BlockSpec(memory_space=pltpu.VMEM)
ANY = pl.BlockSpec(memory_space=pl.ANY)
SMEM = pl.BlockSpec(memory_space=pltpu.SMEM)


def lane_index(shape):
    return lax.broadcasted_iota(jnp.int32, shape, len(shape) - 1)


def barrel(vectors, position):
    count = len(vectors)
    step = 1
    while step < count:
        mask = (position & step) != 0
        vectors = [jnp.where(mask, vectors[(n + step) % count], vectors[n]) for n in range(count)]
        step *= 2
    return vectors


def whiten_kernel(
    x_hbm,
    mask_hbm,
    out_hbm,
    x_ref,
    mask_ref,
    rows_ref,
    factor_ref,
    valid_ref,
    out_ref,
    in_sem,
    mask_sem,
    out_sem,
):
    def read(h):
        here = x_hbm.at[pl.ds(h * S_BLK * 64, S_BLK * 64)]
        return pltpu.make_async_copy(here, x_ref.at[h], in_sem.at[h])

    def write(q):
        here = pl.ds(q * QUARTER, QUARTER)
        return pltpu.make_async_copy(out_ref.at[here], out_hbm.at[here], out_sem.at[q])

    mask_copy = pltpu.make_async_copy(mask_hbm, mask_ref, mask_sem)
    mask_copy.start()
    for h in range(HOURS):
        read(h).start()
    mask_copy.wait()
    eye = lax.broadcasted_iota(jnp.int32, (S_BLK, S_BLK), 0) == lane_index((S_BLK, S_BLK))
    for h in range(HOURS):
        valid = jnp.broadcast_to(mask_ref[h : h + 1, :].astype(jnp.float32), (S_BLK, S_BLK))
        valid = jnp.sum(jnp.where(eye, valid, 0.0), axis=1, keepdims=True)
        valid_ref[h * S_BLK : (h + 1) * S_BLK, :] = jnp.broadcast_to(valid, (S_BLK, LANES))
    for h in range(HOURS):
        read(h).wait()
        totals = []
        for s in range(S_BLK):
            wide = x_ref[h, s * 64 : (s + 1) * 64, :].astype(jnp.float32)
            rows_ref[h, s * PITCH : s * PITCH + 64, :] = wide
            squares = wide * wide
            total = squares[0:8]
            for r in range(1, 8):
                total = total + squares[r * 8 : (r + 1) * 8]
            totals.append(jnp.sum(total, axis=0, keepdims=True))
        factor_ref[h * S_BLK : (h + 1) * S_BLK, :] = jnp.concatenate(totals, axis=0)
    power = jnp.sum(factor_ref[...], axis=1, keepdims=True) * (1.0 / F)
    power = jnp.broadcast_to(power, (HOURS * S_BLK, LANES))
    factor_ref[...] = valid_ref[...] / jnp.sqrt(power + 1e-06)
    position = lane_index((S_BLK, LANES)) // BINS

    def quarter(q, carry):
        for part in range(16):
            rolled = []
            for h in range(HOURS):
                wide = rows_ref[h, pl.ds(q * 16 + part, S_BLK, stride=PITCH), :]
                value = (wide * factor_ref[h * S_BLK : (h + 1) * S_BLK, :]).astype(jnp.bfloat16)
                rolled.append(pltpu.roll(value, BINS * h, 1) if h else value)
            mixed = barrel(rolled, position)
            for g in range(GROUPS):
                row = (part // 2 * GROUPS + g) * (2 * S_BLK) + part % 2 * S_BLK
                row = pl.multiple_of(q * QUARTER + row, S_BLK)
                out_ref[pl.ds(row, S_BLK), :] = mixed[(-g) % GROUPS]
        write(q).start()
        return carry

    lax.fori_loop(0, 4, quarter, 0)
    for q in range(4):
        write(q).wait()


def cross_kernel(pairs_ref, x_ref, out_ref, whole_ref, keep_ref, place_ref, flat_ref):
    position = lane_index((S_BLK, LANES)) % BINS
    for b in range(BLOCKS):
        for c in range(2):
            rolled = []
            for d in range(DAYS):
                row = (b * DAYS + d) * (2 * S_BLK) + c * S_BLK
                value = x_ref[row : row + S_BLK, :]
                rolled.append(pltpu.roll(value, d, 1) if d else value)
            mixed = barrel(rolled, position)
            for u in range(BINS):
                whole_ref[u, b * S_BLK : (b + 1) * S_BLK, c * LANES : (c + 1) * LANES] = mixed[
                    (-u) % BINS
                ]
    owner = lane_index((S_BLK, 256)) // S_BLK
    for p in range(PAIRS):
        kept = (owner == pairs_ref[p, 1]).astype(jnp.float32)
        keep_ref[p * S_BLK : (p + 1) * S_BLK, :] = kept.astype(jnp.bfloat16)
    from_j = lax.broadcasted_iota(jnp.int32, (LANES, LANES), 0) % S_BLK
    to_lane = lane_index((LANES, LANES))
    for n in range(8):
        placed = (to_lane == from_j + n * S_BLK).astype(jnp.float32)
        place_ref[n * LANES : (n + 1) * LANES, :] = placed.astype(jnp.bfloat16)
    firsts = [pl.multiple_of(pairs_ref[p, 0] * S_BLK, S_BLK) for p in range(PAIRS)]
    for t in range(4):
        folded = []
        for uu in range(4):
            u = t * 4 + uu
            re, im = (
                jnp.concatenate(
                    [whole_ref[u, pl.ds(first, S_BLK), c * LANES : (c + 1) * LANES] for first in firsts],
                    axis=0,
                )
                for c in range(2)
            )
            right = whole_ref[u]
            for c in range(2):
                left = jnp.concatenate([im, -re] if c else [re, im], axis=1)
                gram = lax.dot_general(
                    left, right, (((1,), (1,)), ((), ())), preferred_element_type=jnp.float32
                )
                kept = gram.astype(jnp.bfloat16) * keep_ref[...]
                folded.append(kept[:, :LANES] + kept[:, LANES:])
        flat_ref[pl.ds(t, 256, stride=4), :] = jnp.dot(
            jnp.concatenate(folded, axis=1), place_ref[...], preferred_element_type=jnp.float32
        )
    out_ref[...] = flat_ref[...].astype(jnp.bfloat16)


def lag_kernel(x_ref, high_ref, low_ref, cos_ref, sin_ref, out_ref, flat_ref):
    flat_ref[...] = x_ref[...].astype(jnp.float32)
    sums = [jnp.zeros((S_BLK, COARSE), jnp.float32) for _ in range(4)]
    for t in range(4):
        part = flat_ref[pl.ds(t, 256, stride=4), :].T.astype(jnp.bfloat16)
        both = jnp.dot(part, high_ref[...], preferred_element_type=jnp.float32) + jnp.dot(
            part, low_ref[...], preferred_element_type=jnp.float32
        )
        for uu in range(4):
            re = both[uu * 32 : uu * 32 + 16]
            im = both[uu * 32 + 16 : uu * 32 + 32]
            sum_re = re[:, :COARSE] - im[:, COARSE:]
            sum_im = re[:, COARSE:] + im[:, :COARSE]
            for w in range(4):
                row = (t * 4 + uu) * 4 + w
                sums[w] = sums[w] + (
                    sum_re * cos_ref[row : row + 1, :] - sum_im * sin_ref[row : row + 1, :]
                )
    for w in range(4):
        out_ref[:, w * COARSE : (w + 1) * COARSE] = sums[w]


def coarse_tables():
    turns = jnp.arange(256, dtype=jnp.int32)[:, None] * jnp.arange(COARSE, dtype=jnp.int32)[None, :]
    phase = jnp.mod(turns, COARSE).astype(jnp.float32) * (2 * math.pi / COARSE)
    table = jnp.concatenate([jnp.cos(phase), jnp.sin(phase)], axis=1)
    high = lax.reduce_precision(table, 8, 7)
    return high.astype(jnp.bfloat16), (table - high).astype(jnp.bfloat16)


def fine_tables(scale):
    shift = (
        jnp.arange(4, dtype=jnp.int32)[:, None] * COARSE
        + jnp.arange(COARSE, dtype=jnp.int32)[None, :]
        - LAGS // 2
    )
    turns = (jnp.arange(BINS, dtype=jnp.int32) + 1)[:, None, None] * shift[None]
    phase = jnp.mod(turns, 2 * F).astype(jnp.float32) * (math.pi / F)
    phase = phase.reshape(BINS * 4, COARSE)
    return jnp.cos(phase) * scale, jnp.sin(phase) * scale


def shards(spectra, hour_mask, pairs):
    values = spectra.reshape(HOURS, S_BLK, 2, TILES, LANES).transpose(0, 1, 3, 2, 4)
    values = values.reshape(HOURS * S_BLK * TILES * 2, LANES)
    whitened = pl.pallas_call(
        whiten_kernel,
        out_shape=jax.ShapeDtypeStruct((DEVICES * 2 * S_BLK, LANES), jnp.bfloat16),
        in_specs=[ANY, ANY],
        out_specs=ANY,
        scratch_shapes=[
            pltpu.VMEM((HOURS, S_BLK * 64, LANES), jnp.bfloat16),
            pltpu.VMEM((HOURS, S_BLK), jnp.int32),
            pltpu.VMEM((HOURS, S_BLK * PITCH, LANES), jnp.float32),
            pltpu.VMEM((HOURS * S_BLK, LANES), jnp.float32),
            pltpu.VMEM((HOURS * S_BLK, LANES), jnp.float32),
            pltpu.VMEM((DEVICES * 2 * S_BLK, LANES), jnp.bfloat16),
            pltpu.SemaphoreType.DMA((HOURS,)),
            pltpu.SemaphoreType.DMA,
            pltpu.SemaphoreType.DMA((4,)),
        ],
        compiler_params=pltpu.CompilerParams(vmem_limit_bytes=60 * 1024 * 1024),
        name="whiten",
    )(values, hour_mask[0])
    spread = lax.all_to_all(
        whitened.reshape(DEVICES, 2 * S_BLK, LANES), BOTH, split_axis=0, concat_axis=0, tiled=True
    )
    cross = pl.pallas_call(
        cross_kernel,
        out_shape=jax.ShapeDtypeStruct((DEVICES * 4, LANES), jnp.bfloat16),
        in_specs=[SMEM, VMEM],
        out_specs=VMEM,
        scratch_shapes=[
            pltpu.VMEM((BINS, 256, 256), jnp.bfloat16),
            pltpu.VMEM((256, 256), jnp.bfloat16),
            pltpu.VMEM((8 * LANES, LANES), jnp.bfloat16),
            pltpu.VMEM((DEVICES * 4, LANES), jnp.float32),
        ],
        compiler_params=pltpu.CompilerParams(vmem_limit_bytes=40 * 1024 * 1024),
        name="cross",
    )(pairs, spread.reshape(DEVICES * 2 * S_BLK, LANES))
    owned = lax.all_to_all(
        cross.reshape(DEVICES, 4, LANES), BOTH, split_axis=0, concat_axis=0, tiled=True
    )
    high, low = coarse_tables()
    cos_fine, sin_fine = fine_tables(1.0 / math.sqrt(F * HOURS * DAYS))
    result = pl.pallas_call(
        lag_kernel,
        out_shape=jax.ShapeDtypeStruct((S_BLK, LAGS), jnp.float32),
        in_specs=[VMEM] * 5,
        out_specs=VMEM,
        scratch_shapes=[pltpu.VMEM((DEVICES * 4, LANES), jnp.float32)],
        compiler_params=pltpu.CompilerParams(vmem_limit_bytes=40 * 1024 * 1024),
        name="lag",
    )(owned.reshape(DEVICES * 4, LANES), high, low, cos_fine, sin_fine)
    return result.reshape(1, S_BLK, LAGS)


def solution(mesh):
    in_specs = (P("day", None, "block", None, None), P("day", None, "block"), P())
    out_specs = P("block", "day", None)
    return jax.shard_map(shards, mesh=mesh, in_specs=in_specs, out_specs=out_specs, check_vma=False)
```

```python
import math

import jax
import jax.numpy as jnp
import ml_dtypes
import numpy as np
from jax import lax
from jax.experimental import pallas as pl
from jax.experimental.pallas import tpu as pltpu
from jax.sharding import PartitionSpec as P

F = 4096
LAGS = 2048
S_BLK = 16
HOURS = 8
DAYS = 16
BLOCKS = 16
PAIRS = 16
LANES = 128
TILES = F // LANES
GROUPS = 8
BINS = 16
DEVICES = 256
COARSE = 512
PITCH = 72
QUARTER = DEVICES * 2 * S_BLK // 4
BOTH = ("block", "day")
VMEM = pl.BlockSpec(memory_space=pltpu.VMEM)
ANY = pl.BlockSpec(memory_space=pl.ANY)
SMEM = pl.BlockSpec(memory_space=pltpu.SMEM)


def lane_index(shape):
    return lax.broadcasted_iota(jnp.int32, shape, len(shape) - 1)


def barrel(vectors, position):
    count = len(vectors)
    step = 1
    while step < count:
        mask = (position & step) != 0
        vectors = [jnp.where(mask, vectors[(n + step) % count], vectors[n]) for n in range(count)]
        step *= 2
    return vectors


def whiten_kernel(
    x_hbm,
    mask_hbm,
    out_hbm,
    x_ref,
    mask_ref,
    rows_ref,
    factor_ref,
    valid_ref,
    out_ref,
    in_sem,
    mask_sem,
    out_sem,
):
    def read(h):
        here = x_hbm.at[pl.ds(h * S_BLK * 64, S_BLK * 64)]
        return pltpu.make_async_copy(here, x_ref.at[h], in_sem.at[h])

    def write(q):
        here = pl.ds(q * QUARTER, QUARTER)
        return pltpu.make_async_copy(out_ref.at[here], out_hbm.at[here], out_sem.at[q])

    mask_copy = pltpu.make_async_copy(mask_hbm, mask_ref, mask_sem)
    mask_copy.start()
    for h in range(HOURS):
        read(h).start()
    mask_copy.wait()
    eye = lax.broadcasted_iota(jnp.int32, (S_BLK, S_BLK), 0) == lane_index((S_BLK, S_BLK))
    for h in range(HOURS):
        valid = jnp.broadcast_to(mask_ref[h : h + 1, :].astype(jnp.float32), (S_BLK, S_BLK))
        valid = jnp.sum(jnp.where(eye, valid, 0.0), axis=1, keepdims=True)
        valid_ref[h * S_BLK : (h + 1) * S_BLK, :] = jnp.broadcast_to(valid, (S_BLK, LANES))
    for h in range(HOURS):
        read(h).wait()
        totals = []
        for s in range(S_BLK):
            wide = x_ref[h, s * 64 : (s + 1) * 64, :].astype(jnp.float32)
            rows_ref[h, s * PITCH : s * PITCH + 64, :] = wide
            squares = wide * wide
            total = squares[0:8]
            for r in range(1, 8):
                total = total + squares[r * 8 : (r + 1) * 8]
            totals.append(jnp.sum(total, axis=0, keepdims=True))
        factor_ref[h * S_BLK : (h + 1) * S_BLK, :] = jnp.concatenate(totals, axis=0)
    power = jnp.sum(factor_ref[...], axis=1, keepdims=True) * (1.0 / F)
    power = jnp.broadcast_to(power, (HOURS * S_BLK, LANES))
    factor_ref[...] = valid_ref[...] / jnp.sqrt(power + 1e-06)
    position = lane_index((S_BLK, LANES)) // BINS

    def quarter(q, carry):
        for part in range(16):
            rolled = []
            for h in range(HOURS):
                wide = rows_ref[h, pl.ds(q * 16 + part, S_BLK, stride=PITCH), :]
                value = (wide * factor_ref[h * S_BLK : (h + 1) * S_BLK, :]).astype(jnp.bfloat16)
                rolled.append(pltpu.roll(value, BINS * h, 1) if h else value)
            mixed = barrel(rolled, position)
            for g in range(GROUPS):
                row = (part // 2 * GROUPS + g) * (2 * S_BLK) + part % 2 * S_BLK
                row = pl.multiple_of(q * QUARTER + row, S_BLK)
                out_ref[pl.ds(row, S_BLK), :] = mixed[(-g) % GROUPS]
        write(q).start()
        return carry

    lax.fori_loop(0, 4, quarter, 0)
    for q in range(4):
        write(q).wait()


def cross_kernel(pairs_ref, x_ref, out_ref, whole_ref, keep_ref, place_ref, flat_ref):
    position = lane_index((S_BLK, LANES)) % BINS
    for b in range(BLOCKS):
        for c in range(2):
            rolled = []
            for d in range(DAYS):
                row = (b * DAYS + d) * (2 * S_BLK) + c * S_BLK
                value = x_ref[row : row + S_BLK, :]
                rolled.append(pltpu.roll(value, d, 1) if d else value)
            mixed = barrel(rolled, position)
            for u in range(BINS):
                whole_ref[u, b * S_BLK : (b + 1) * S_BLK, c * LANES : (c + 1) * LANES] = mixed[
                    (-u) % BINS
                ]
    owner = lane_index((S_BLK, 256)) // S_BLK
    for p in range(PAIRS):
        kept = (owner == pairs_ref[1, p]).astype(jnp.float32)
        keep_ref[p * S_BLK : (p + 1) * S_BLK, :] = kept.astype(jnp.bfloat16)
    from_j = lax.broadcasted_iota(jnp.int32, (LANES, LANES), 0) % S_BLK
    to_lane = lane_index((LANES, LANES))
    for n in range(8):
        placed = (to_lane == from_j + n * S_BLK).astype(jnp.float32)
        place_ref[n * LANES : (n + 1) * LANES, :] = placed.astype(jnp.bfloat16)
    firsts = [pl.multiple_of(pairs_ref[0, p] * S_BLK, S_BLK) for p in range(PAIRS)]
    for t in range(4):
        folded = []
        for uu in range(4):
            u = t * 4 + uu
            re, im = (
                jnp.concatenate(
                    [whole_ref[u, pl.ds(first, S_BLK), c * LANES : (c + 1) * LANES] for first in firsts],
                    axis=0,
                )
                for c in range(2)
            )
            right = whole_ref[u]
            for c in range(2):
                left = jnp.concatenate([im, -re] if c else [re, im], axis=1)
                gram = lax.dot_general(
                    left, right, (((1,), (1,)), ((), ())), preferred_element_type=jnp.float32
                )
                kept = gram.astype(jnp.bfloat16) * keep_ref[...]
                folded.append(kept[:, :LANES] + kept[:, LANES:])
        flat_ref[pl.ds(t, 256, stride=4), :] = jnp.dot(
            jnp.concatenate(folded, axis=1), place_ref[...], preferred_element_type=jnp.float32
        )
    out_ref[...] = flat_ref[...].astype(jnp.bfloat16)


def lag_kernel(x_ref, high_ref, low_ref, cos_ref, sin_ref, out_ref, flat_ref):
    flat_ref[...] = x_ref[...].astype(jnp.float32)
    sums = [jnp.zeros((S_BLK, COARSE), jnp.float32) for _ in range(4)]
    for t in range(4):
        part = flat_ref[pl.ds(t, 256, stride=4), :].T.astype(jnp.bfloat16)
        both = jnp.dot(part, high_ref[...], preferred_element_type=jnp.float32) + jnp.dot(
            part, low_ref[...], preferred_element_type=jnp.float32
        )
        for uu in range(4):
            re = both[uu * 32 : uu * 32 + 16]
            im = both[uu * 32 + 16 : uu * 32 + 32]
            sum_re = re[:, :COARSE] - im[:, COARSE:]
            sum_im = re[:, COARSE:] + im[:, :COARSE]
            for w in range(4):
                row = (t * 4 + uu) * 4 + w
                sums[w] = sums[w] + (
                    sum_re * cos_ref[row : row + 1, :] - sum_im * sin_ref[row : row + 1, :]
                )
    for w in range(4):
        out_ref[:, w * COARSE : (w + 1) * COARSE] = sums[w]


def coarse_tables():
    turns = np.arange(256)[:, None] * np.arange(COARSE)[None, :] % COARSE
    phase = turns * (2 * math.pi / COARSE)
    table = np.concatenate([np.cos(phase), np.sin(phase)], axis=1).astype(np.float32)
    high = table.astype(ml_dtypes.bfloat16)
    return high, (table - high.astype(np.float32)).astype(ml_dtypes.bfloat16)


def fine_tables(scale):
    shift = np.arange(4)[:, None] * COARSE + np.arange(COARSE)[None, :] - LAGS // 2
    turns = (np.arange(BINS) + 1)[:, None, None] * shift[None] % (2 * F)
    phase = (turns * (math.pi / F)).reshape(BINS * 4, COARSE)
    return (np.cos(phase) * scale).astype(np.float32), (np.sin(phase) * scale).astype(np.float32)


def shards(spectra, hour_mask, pairs):
    values = spectra.reshape(HOURS, S_BLK, 2, TILES, LANES).transpose(0, 1, 3, 2, 4)
    values = values.reshape(HOURS * S_BLK * TILES * 2, LANES)
    whitened = pl.pallas_call(
        whiten_kernel,
        out_shape=jax.ShapeDtypeStruct((DEVICES * 2 * S_BLK, LANES), jnp.bfloat16),
        in_specs=[ANY, ANY],
        out_specs=ANY,
        scratch_shapes=[
            pltpu.VMEM((HOURS, S_BLK * 64, LANES), jnp.bfloat16),
            pltpu.VMEM((HOURS, S_BLK), jnp.int32),
            pltpu.VMEM((HOURS, S_BLK * PITCH, LANES), jnp.float32),
            pltpu.VMEM((HOURS * S_BLK, LANES), jnp.float32),
            pltpu.VMEM((HOURS * S_BLK, LANES), jnp.float32),
            pltpu.VMEM((DEVICES * 2 * S_BLK, LANES), jnp.bfloat16),
            pltpu.SemaphoreType.DMA((HOURS,)),
            pltpu.SemaphoreType.DMA,
            pltpu.SemaphoreType.DMA((4,)),
        ],
        compiler_params=pltpu.CompilerParams(vmem_limit_bytes=60 * 1024 * 1024),
        name="whiten",
    )(values, hour_mask[0])
    spread = lax.all_to_all(
        whitened.reshape(DEVICES, 2 * S_BLK, LANES), BOTH, split_axis=0, concat_axis=0, tiled=True
    )
    cross = pl.pallas_call(
        cross_kernel,
        out_shape=jax.ShapeDtypeStruct((DEVICES * 4, LANES), jnp.bfloat16),
        in_specs=[SMEM, VMEM],
        out_specs=VMEM,
        scratch_shapes=[
            pltpu.VMEM((BINS, 256, 256), jnp.bfloat16),
            pltpu.VMEM((256, 256), jnp.bfloat16),
            pltpu.VMEM((8 * LANES, LANES), jnp.bfloat16),
            pltpu.VMEM((DEVICES * 4, LANES), jnp.float32),
        ],
        compiler_params=pltpu.CompilerParams(vmem_limit_bytes=40 * 1024 * 1024),
        name="cross",
    )(pairs.T, spread.reshape(DEVICES * 2 * S_BLK, LANES))
    owned = lax.all_to_all(
        cross.reshape(DEVICES, 4, LANES), BOTH, split_axis=0, concat_axis=0, tiled=True
    )
    high, low = coarse_tables()
    cos_fine, sin_fine = fine_tables(1.0 / math.sqrt(F * HOURS * DAYS))
    result = pl.pallas_call(
        lag_kernel,
        out_shape=jax.ShapeDtypeStruct((S_BLK, LAGS), jnp.float32),
        in_specs=[VMEM] * 5,
        out_specs=VMEM,
        scratch_shapes=[pltpu.VMEM((DEVICES * 4, LANES), jnp.float32)],
        compiler_params=pltpu.CompilerParams(vmem_limit_bytes=40 * 1024 * 1024),
        name="lag",
    )(owned.reshape(DEVICES * 4, LANES), high, low, cos_fine, sin_fine)
    return result.reshape(1, S_BLK, LAGS)


def solution(mesh):
    in_specs = (P("day", None, "block", None, None), P("day", None, "block"), P())
    out_specs = P("block", "day", None)
    return jax.shard_map(shards, mesh=mesh, in_specs=in_specs, out_specs=out_specs, check_vma=False)
```

```python
import math

import jax
import jax.numpy as jnp
import ml_dtypes
import numpy as np
from jax import lax
from jax.experimental import pallas as pl
from jax.experimental.pallas import tpu as pltpu
from jax.sharding import PartitionSpec as P

F = 4096
LAGS = 2048
S_BLK = 16
HOURS = 8
DAYS = 16
BLOCKS = 16
PAIRS = 16
LANES = 128
TILES = F // LANES
GROUPS = 8
BINS = 16
DEVICES = 256
COARSE = 512
PITCH = 72
QUARTER = DEVICES * 2 * S_BLK // 4
BOTH = ("block", "day")
VMEM = pl.BlockSpec(memory_space=pltpu.VMEM)
HBM = pl.BlockSpec(memory_space=pltpu.HBM)
SMEM = pl.BlockSpec(memory_space=pltpu.SMEM)


def lane_index(shape):
    return lax.broadcasted_iota(jnp.int32, shape, len(shape) - 1)


def barrel(vectors, position):
    count = len(vectors)
    step = 1
    while step < count:
        mask = (position & step) != 0
        vectors = [jnp.where(mask, vectors[(n + step) % count], vectors[n]) for n in range(count)]
        step *= 2
    return vectors


def whiten_kernel(
    x_hbm,
    mask_hbm,
    out_ref,
    x_ref,
    mask_ref,
    rows_ref,
    factor_ref,
    valid_ref,
    in_sem,
    mask_sem,
):
    def read(h):
        here = x_hbm.at[pl.ds(h * S_BLK * 64, S_BLK * 64)]
        return pltpu.make_async_copy(here, x_ref.at[h], in_sem.at[h])

    mask_copy = pltpu.make_async_copy(mask_hbm, mask_ref, mask_sem)
    mask_copy.start()
    for h in range(HOURS):
        read(h).start()
    mask_copy.wait()
    eye = lax.broadcasted_iota(jnp.int32, (S_BLK, S_BLK), 0) == lane_index((S_BLK, S_BLK))
    for h in range(HOURS):
        valid = jnp.broadcast_to(mask_ref[h : h + 1, :].astype(jnp.float32), (S_BLK, S_BLK))
        valid = jnp.sum(jnp.where(eye, valid, 0.0), axis=1, keepdims=True)
        valid_ref[h * S_BLK : (h + 1) * S_BLK, :] = jnp.broadcast_to(valid, (S_BLK, LANES))
    for h in range(HOURS):
        read(h).wait()
        totals = []
        for s in range(S_BLK):
            wide = x_ref[h, s * 64 : (s + 1) * 64, :].astype(jnp.float32)
            rows_ref[h, s * PITCH : s * PITCH + 64, :] = wide
            squares = wide * wide
            total = squares[0:8]
            for r in range(1, 8):
                total = total + squares[r * 8 : (r + 1) * 8]
            totals.append(jnp.sum(total, axis=0, keepdims=True))
        factor_ref[h * S_BLK : (h + 1) * S_BLK, :] = jnp.concatenate(totals, axis=0)
    power = jnp.sum(factor_ref[...], axis=1, keepdims=True) * (1.0 / F)
    power = jnp.broadcast_to(power, (HOURS * S_BLK, LANES))
    factor_ref[...] = valid_ref[...] / jnp.sqrt(power + 1e-06)
    position = lane_index((S_BLK, LANES)) // BINS

    def quarter(q, carry):
        for part in range(16):
            rolled = []
            for h in range(HOURS):
                wide = rows_ref[h, pl.ds(q * 16 + part, S_BLK, stride=PITCH), :]
                value = (wide * factor_ref[h * S_BLK : (h + 1) * S_BLK, :]).astype(jnp.bfloat16)
                rolled.append(pltpu.roll(value, BINS * h, 1) if h else value)
            mixed = barrel(rolled, position)
            for g in range(GROUPS):
                row = (part // 2 * GROUPS + g) * (2 * S_BLK) + part % 2 * S_BLK
                row = pl.multiple_of(q * QUARTER + row, S_BLK)
                out_ref[pl.ds(row, S_BLK), :] = mixed[(-g) % GROUPS]
        return carry

    lax.fori_loop(0, 4, quarter, 0)


def cross_kernel(pairs_ref, x_ref, out_ref, whole_ref, keep_ref, place_ref, flat_ref):
    position = lane_index((S_BLK, LANES)) % BINS
    for b in range(BLOCKS):
        for c in range(2):
            rolled = []
            for d in range(DAYS):
                row = (b * DAYS + d) * (2 * S_BLK) + c * S_BLK
                value = x_ref[row : row + S_BLK, :]
                rolled.append(pltpu.roll(value, d, 1) if d else value)
            mixed = barrel(rolled, position)
            for u in range(BINS):
                whole_ref[u, b * S_BLK : (b + 1) * S_BLK, c * LANES : (c + 1) * LANES] = mixed[
                    (-u) % BINS
                ]
    owner = lane_index((S_BLK, 256)) // S_BLK
    for p in range(PAIRS):
        kept = (owner == pairs_ref[1, p]).astype(jnp.float32)
        keep_ref[p * S_BLK : (p + 1) * S_BLK, :] = kept.astype(jnp.bfloat16)
    from_j = lax.broadcasted_iota(jnp.int32, (LANES, LANES), 0) % S_BLK
    to_lane = lane_index((LANES, LANES))
    for n in range(8):
        placed = (to_lane == from_j + n * S_BLK).astype(jnp.float32)
        place_ref[n * LANES : (n + 1) * LANES, :] = placed.astype(jnp.bfloat16)
    firsts = [pl.multiple_of(pairs_ref[0, p] * S_BLK, S_BLK) for p in range(PAIRS)]
    for t in range(4):
        folded = []
        for uu in range(4):
            u = t * 4 + uu
            re, im = (
                jnp.concatenate(
                    [whole_ref[u, pl.ds(first, S_BLK), c * LANES : (c + 1) * LANES] for first in firsts],
                    axis=0,
                )
                for c in range(2)
            )
            right = whole_ref[u]
            for c in range(2):
                left = jnp.concatenate([im, -re] if c else [re, im], axis=1)
                gram = lax.dot_general(
                    left, right, (((1,), (1,)), ((), ())), preferred_element_type=jnp.float32
                )
                kept = gram.astype(jnp.bfloat16) * keep_ref[...]
                folded.append(kept[:, :LANES] + kept[:, LANES:])
        flat_ref[pl.ds(t, 256, stride=4), :] = jnp.dot(
            jnp.concatenate(folded, axis=1), place_ref[...], preferred_element_type=jnp.float32
        )
    out_ref[...] = flat_ref[...].astype(jnp.bfloat16)


def lag_kernel(x_ref, high_ref, low_ref, cos_ref, sin_ref, out_ref, flat_ref):
    flat_ref[...] = x_ref[...].astype(jnp.float32)
    sums = [jnp.zeros((S_BLK, COARSE), jnp.float32) for _ in range(4)]
    for t in range(4):
        part = flat_ref[pl.ds(t, 256, stride=4), :].T.astype(jnp.bfloat16)
        both = jnp.dot(part, high_ref[...], preferred_element_type=jnp.float32) + jnp.dot(
            part, low_ref[...], preferred_element_type=jnp.float32
        )
        for uu in range(4):
            re = both[uu * 32 : uu * 32 + 16]
            im = both[uu * 32 + 16 : uu * 32 + 32]
            sum_re = re[:, :COARSE] - im[:, COARSE:]
            sum_im = re[:, COARSE:] + im[:, :COARSE]
            for w in range(4):
                row = (t * 4 + uu) * 4 + w
                sums[w] = sums[w] + (
                    sum_re * cos_ref[row : row + 1, :] - sum_im * sin_ref[row : row + 1, :]
                )
    for w in range(4):
        out_ref[:, w * COARSE : (w + 1) * COARSE] = sums[w]


def coarse_tables():
    turns = np.arange(256)[:, None] * np.arange(COARSE)[None, :] % COARSE
    phase = turns * (2 * math.pi / COARSE)
    table = np.concatenate([np.cos(phase), np.sin(phase)], axis=1).astype(np.float32)
    high = table.astype(ml_dtypes.bfloat16)
    return high, (table - high.astype(np.float32)).astype(ml_dtypes.bfloat16)


def fine_tables(scale):
    shift = np.arange(4)[:, None] * COARSE + np.arange(COARSE)[None, :] - LAGS // 2
    turns = (np.arange(BINS) + 1)[:, None, None] * shift[None] % (2 * F)
    phase = (turns * (math.pi / F)).reshape(BINS * 4, COARSE)
    return (np.cos(phase) * scale).astype(np.float32), (np.sin(phase) * scale).astype(np.float32)


def shards(spectra, hour_mask, pairs):
    values = spectra.reshape(HOURS, S_BLK, 2, TILES, LANES).transpose(0, 1, 3, 2, 4)
    values = values.reshape(HOURS * S_BLK * TILES * 2, LANES)
    whitened = pl.pallas_call(
        whiten_kernel,
        out_shape=jax.ShapeDtypeStruct((DEVICES * 2 * S_BLK, LANES), jnp.bfloat16),
        in_specs=[HBM, HBM],
        out_specs=VMEM,
        scratch_shapes=[
            pltpu.VMEM((HOURS, S_BLK * 64, LANES), jnp.bfloat16),
            pltpu.VMEM((HOURS, S_BLK), jnp.int32),
            pltpu.VMEM((HOURS, S_BLK * PITCH, LANES), jnp.float32),
            pltpu.VMEM((HOURS * S_BLK, LANES), jnp.float32),
            pltpu.VMEM((HOURS * S_BLK, LANES), jnp.float32),
            pltpu.SemaphoreType.DMA((HOURS,)),
            pltpu.SemaphoreType.DMA,
        ],
        compiler_params=pltpu.CompilerParams(vmem_limit_bytes=50 * 1024 * 1024),
        name="whiten",
    )(values, hour_mask[0])
    spread = lax.all_to_all(
        whitened.reshape(DEVICES, 2 * S_BLK, LANES), BOTH, split_axis=0, concat_axis=0, tiled=True
    )
    cross = pl.pallas_call(
        cross_kernel,
        out_shape=jax.ShapeDtypeStruct((DEVICES * 4, LANES), jnp.bfloat16),
        in_specs=[SMEM, VMEM],
        out_specs=VMEM,
        scratch_shapes=[
            pltpu.VMEM((BINS, 256, 256), jnp.bfloat16),
            pltpu.VMEM((256, 256), jnp.bfloat16),
            pltpu.VMEM((8 * LANES, LANES), jnp.bfloat16),
            pltpu.VMEM((DEVICES * 4, LANES), jnp.float32),
        ],
        compiler_params=pltpu.CompilerParams(vmem_limit_bytes=40 * 1024 * 1024),
        name="cross",
    )(pairs.T, spread.reshape(DEVICES * 2 * S_BLK, LANES))
    owned = lax.all_to_all(
        cross.reshape(DEVICES, 4, LANES), BOTH, split_axis=0, concat_axis=0, tiled=True
    )
    high, low = coarse_tables()
    cos_fine, sin_fine = fine_tables(1.0 / math.sqrt(F * HOURS * DAYS))
    result = pl.pallas_call(
        lag_kernel,
        out_shape=jax.ShapeDtypeStruct((S_BLK, LAGS), jnp.float32),
        in_specs=[VMEM] * 5,
        out_specs=VMEM,
        scratch_shapes=[pltpu.VMEM((DEVICES * 4, LANES), jnp.float32)],
        compiler_params=pltpu.CompilerParams(vmem_limit_bytes=40 * 1024 * 1024),
        name="lag",
    )(owned.reshape(DEVICES * 4, LANES), high, low, cos_fine, sin_fine)
    return result.reshape(1, S_BLK, LAGS)


def solution(mesh):
    in_specs = (P("day", None, "block", None, None), P("day", None, "block"), P())
    out_specs = P("block", "day", None)
    return jax.shard_map(shards, mesh=mesh, in_specs=in_specs, out_specs=out_specs, check_vma=False)
```

```python
import math

import jax
import jax.numpy as jnp
import ml_dtypes
import numpy as np
from jax import lax
from jax.experimental import pallas as pl
from jax.experimental.pallas import tpu as pltpu
from jax.sharding import PartitionSpec as P

F = 4096
LAGS = 2048
S_BLK = 16
HOURS = 8
DAYS = 16
BLOCKS = 16
PAIRS = 16
LANES = 128
TILES = F // LANES
GROUPS = 8
BINS = 16
DEVICES = 256
COARSE = 512
PITCH = 72
QUARTER = DEVICES * 2 * S_BLK // 4
BOTH = ("block", "day")
VMEM = pl.BlockSpec(memory_space=pltpu.VMEM)
HBM = pl.BlockSpec(memory_space=pltpu.HBM)
SMEM = pl.BlockSpec(memory_space=pltpu.SMEM)


def lane_index(shape):
    return lax.broadcasted_iota(jnp.int32, shape, len(shape) - 1)


def barrel(vectors, position):
    count = len(vectors)
    step = 1
    while step < count:
        mask = (position & step) != 0
        vectors = [jnp.where(mask, vectors[(n + step) % count], vectors[n]) for n in range(count)]
        step *= 2
    return vectors


def whiten_kernel(
    x_hbm,
    mask_hbm,
    out_ref,
    x_ref,
    mask_ref,
    rows_ref,
    factor_ref,
    valid_ref,
    in_sem,
    mask_sem,
):
    def read(h):
        here = x_hbm.at[pl.ds(h * S_BLK * 64, S_BLK * 64)]
        return pltpu.make_async_copy(here, x_ref.at[h], in_sem.at[h])

    mask_copy = pltpu.make_async_copy(mask_hbm, mask_ref, mask_sem)
    mask_copy.start()
    for h in range(HOURS):
        read(h).start()
    mask_copy.wait()
    eye = lax.broadcasted_iota(jnp.int32, (S_BLK, S_BLK), 0) == lane_index((S_BLK, S_BLK))
    for h in range(HOURS):
        valid = jnp.broadcast_to(mask_ref[h : h + 1, :].astype(jnp.float32), (S_BLK, S_BLK))
        valid = jnp.sum(jnp.where(eye, valid, 0.0), axis=1, keepdims=True)
        valid_ref[h * S_BLK : (h + 1) * S_BLK, :] = jnp.broadcast_to(valid, (S_BLK, LANES))
    for h in range(HOURS):
        read(h).wait()
        totals = []
        for s in range(S_BLK):
            wide = x_ref[h, s * 64 : (s + 1) * 64, :].astype(jnp.float32)
            rows_ref[h, s * PITCH : s * PITCH + 64, :] = wide
            squares = wide * wide
            total = squares[0:8]
            for r in range(1, 8):
                total = total + squares[r * 8 : (r + 1) * 8]
            totals.append(jnp.sum(total, axis=0, keepdims=True))
        factor_ref[h * S_BLK : (h + 1) * S_BLK, :] = jnp.concatenate(totals, axis=0)
    power = jnp.sum(factor_ref[...], axis=1, keepdims=True) * (1.0 / F)
    power = jnp.broadcast_to(power, (HOURS * S_BLK, LANES))
    factor_ref[...] = valid_ref[...] / jnp.sqrt(power + 1e-06)
    position = lane_index((S_BLK, LANES)) // BINS

    def quarter(q, carry):
        for part in range(16):
            rolled = []
            for h in range(HOURS):
                wide = rows_ref[h, pl.ds(q * 16 + part, S_BLK, stride=PITCH), :]
                value = (wide * factor_ref[h * S_BLK : (h + 1) * S_BLK, :]).astype(jnp.bfloat16)
                rolled.append(pltpu.roll(value, BINS * h, 1) if h else value)
            mixed = barrel(rolled, position)
            for g in range(GROUPS):
                row = (part // 2 * GROUPS + g) * (2 * S_BLK) + part % 2 * S_BLK
                row = pl.multiple_of(q * QUARTER + row, S_BLK)
                out_ref[pl.ds(row, S_BLK), :] = mixed[(-g) % GROUPS]
        return carry

    for q in range(4):
        quarter(q, 0)


def cross_kernel(pairs_ref, x_ref, out_ref, whole_ref, keep_ref, place_ref, flat_ref):
    position = lane_index((S_BLK, LANES)) % BINS
    for b in range(BLOCKS):
        for c in range(2):
            rolled = []
            for d in range(DAYS):
                row = (b * DAYS + d) * (2 * S_BLK) + c * S_BLK
                value = x_ref[row : row + S_BLK, :]
                rolled.append(pltpu.roll(value, d, 1) if d else value)
            mixed = barrel(rolled, position)
            for u in range(BINS):
                whole_ref[u, b * S_BLK : (b + 1) * S_BLK, c * LANES : (c + 1) * LANES] = mixed[
                    (-u) % BINS
                ]
    owner = lane_index((S_BLK, 256)) // S_BLK
    for p in range(PAIRS):
        kept = (owner == pairs_ref[1, p]).astype(jnp.float32)
        keep_ref[p * S_BLK : (p + 1) * S_BLK, :] = kept.astype(jnp.bfloat16)
    from_j = lax.broadcasted_iota(jnp.int32, (LANES, LANES), 0) % S_BLK
    to_lane = lane_index((LANES, LANES))
    for n in range(8):
        placed = (to_lane == from_j + n * S_BLK).astype(jnp.float32)
        place_ref[n * LANES : (n + 1) * LANES, :] = placed.astype(jnp.bfloat16)
    firsts = [pl.multiple_of(pairs_ref[0, p] * S_BLK, S_BLK) for p in range(PAIRS)]
    for t in range(4):
        folded = []
        for uu in range(4):
            u = t * 4 + uu
            re, im = (
                jnp.concatenate(
                    [whole_ref[u, pl.ds(first, S_BLK), c * LANES : (c + 1) * LANES] for first in firsts],
                    axis=0,
                )
                for c in range(2)
            )
            right = whole_ref[u]
            for c in range(2):
                left = jnp.concatenate([im, -re] if c else [re, im], axis=1)
                gram = lax.dot_general(
                    left, right, (((1,), (1,)), ((), ())), preferred_element_type=jnp.float32
                )
                kept = gram.astype(jnp.bfloat16) * keep_ref[...]
                folded.append(kept[:, :LANES] + kept[:, LANES:])
        flat_ref[pl.ds(t, 256, stride=4), :] = jnp.dot(
            jnp.concatenate(folded, axis=1), place_ref[...], preferred_element_type=jnp.float32
        )
    out_ref[...] = flat_ref[...].astype(jnp.bfloat16)


def lag_kernel(x_ref, high_ref, low_ref, cos_ref, sin_ref, out_ref, flat_ref):
    flat_ref[...] = x_ref[...].astype(jnp.float32)
    sums = [jnp.zeros((S_BLK, COARSE), jnp.float32) for _ in range(4)]
    for t in range(4):
        part = flat_ref[pl.ds(t, 256, stride=4), :].T.astype(jnp.bfloat16)
        both = jnp.dot(part, high_ref[...], preferred_element_type=jnp.float32) + jnp.dot(
            part, low_ref[...], preferred_element_type=jnp.float32
        )
        for uu in range(4):
            re = both[uu * 32 : uu * 32 + 16]
            im = both[uu * 32 + 16 : uu * 32 + 32]
            sum_re = re[:, :COARSE] - im[:, COARSE:]
            sum_im = re[:, COARSE:] + im[:, :COARSE]
            for w in range(4):
                row = (t * 4 + uu) * 4 + w
                sums[w] = sums[w] + (
                    sum_re * cos_ref[row : row + 1, :] - sum_im * sin_ref[row : row + 1, :]
                )
    for w in range(4):
        out_ref[:, w * COARSE : (w + 1) * COARSE] = sums[w]


def coarse_tables():
    turns = np.arange(256)[:, None] * np.arange(COARSE)[None, :] % COARSE
    phase = turns * (2 * math.pi / COARSE)
    table = np.concatenate([np.cos(phase), np.sin(phase)], axis=1).astype(np.float32)
    high = table.astype(ml_dtypes.bfloat16)
    return high, (table - high.astype(np.float32)).astype(ml_dtypes.bfloat16)


def fine_tables(scale):
    shift = np.arange(4)[:, None] * COARSE + np.arange(COARSE)[None, :] - LAGS // 2
    turns = (np.arange(BINS) + 1)[:, None, None] * shift[None] % (2 * F)
    phase = (turns * (math.pi / F)).reshape(BINS * 4, COARSE)
    return (np.cos(phase) * scale).astype(np.float32), (np.sin(phase) * scale).astype(np.float32)


def shards(spectra, hour_mask, pairs):
    values = spectra.reshape(HOURS, S_BLK, 2, TILES, LANES).transpose(0, 1, 3, 2, 4)
    values = values.reshape(HOURS * S_BLK * TILES * 2, LANES)
    whitened = pl.pallas_call(
        whiten_kernel,
        out_shape=jax.ShapeDtypeStruct((DEVICES * 2 * S_BLK, LANES), jnp.bfloat16),
        in_specs=[HBM, HBM],
        out_specs=VMEM,
        scratch_shapes=[
            pltpu.VMEM((HOURS, S_BLK * 64, LANES), jnp.bfloat16),
            pltpu.VMEM((HOURS, S_BLK), jnp.int32),
            pltpu.VMEM((HOURS, S_BLK * PITCH, LANES), jnp.float32),
            pltpu.VMEM((HOURS * S_BLK, LANES), jnp.float32),
            pltpu.VMEM((HOURS * S_BLK, LANES), jnp.float32),
            pltpu.SemaphoreType.DMA((HOURS,)),
            pltpu.SemaphoreType.DMA,
        ],
        compiler_params=pltpu.CompilerParams(vmem_limit_bytes=50 * 1024 * 1024),
        name="whiten",
    )(values, hour_mask[0])
    spread = lax.all_to_all(
        whitened.reshape(DEVICES, 2 * S_BLK, LANES), BOTH, split_axis=0, concat_axis=0, tiled=True
    )
    cross = pl.pallas_call(
        cross_kernel,
        out_shape=jax.ShapeDtypeStruct((DEVICES * 4, LANES), jnp.bfloat16),
        in_specs=[SMEM, VMEM],
        out_specs=VMEM,
        scratch_shapes=[
            pltpu.VMEM((BINS, 256, 256), jnp.bfloat16),
            pltpu.VMEM((256, 256), jnp.bfloat16),
            pltpu.VMEM((8 * LANES, LANES), jnp.bfloat16),
            pltpu.VMEM((DEVICES * 4, LANES), jnp.float32),
        ],
        compiler_params=pltpu.CompilerParams(vmem_limit_bytes=40 * 1024 * 1024),
        name="cross",
    )(pairs.T, spread.reshape(DEVICES * 2 * S_BLK, LANES))
    owned = lax.all_to_all(
        cross.reshape(DEVICES, 4, LANES), BOTH, split_axis=0, concat_axis=0, tiled=True
    )
    high, low = coarse_tables()
    cos_fine, sin_fine = fine_tables(1.0 / math.sqrt(F * HOURS * DAYS))
    result = pl.pallas_call(
        lag_kernel,
        out_shape=jax.ShapeDtypeStruct((S_BLK, LAGS), jnp.float32),
        in_specs=[VMEM] * 5,
        out_specs=VMEM,
        scratch_shapes=[pltpu.VMEM((DEVICES * 4, LANES), jnp.float32)],
        compiler_params=pltpu.CompilerParams(vmem_limit_bytes=40 * 1024 * 1024),
        name="lag",
    )(owned.reshape(DEVICES * 4, LANES), high, low, cos_fine, sin_fine)
    return result.reshape(1, S_BLK, LAGS)


def solution(mesh):
    in_specs = (P("day", None, "block", None, None), P("day", None, "block"), P())
    out_specs = P("block", "day", None)
    return jax.shard_map(shards, mesh=mesh, in_specs=in_specs, out_specs=out_specs, check_vma=False)
```
